256 devices in a mesh: dp: 16 (over x, y_hi, core), ctx: 16 (over y_lo, z).
Axes of the slice: x: 4, y: 4 (y_hi: 2, y_lo: 2; y = y_hi * 2 + y_lo), z: 8, core: 2. Of those that a mesh axis runs over, the one named last changes fastest.
Arguments:
- queries: bfloat16 [16, 16384, 512], P('dp', 'ctx'), may hold values from -6 to 6
- keys: bfloat16 [16, 16384, 128], P('dp', 'ctx'), may hold values from -6 to 6
- values: bfloat16 [16, 16384, 128], P('dp', 'ctx'), may hold values from -6 to 6
- dest_replica: int32 [16, 256], P('dp', 'ctx'), may hold values from 0 to 15, as said below
- dest_slot: int32 [16, 256], P('dp', 'ctx'), may hold values from 0 to 255, as said below
- doc_lengths: int32 [16, 64], P('dp'), may hold values from 1 to 32, 256 in all within a row
- tile_mask: int32 [16, 256, 256], P('dp', 'ctx'), may hold values 0 or 1
Outputs:
- attended: bfloat16 [16, 16384, 512], P('dp', 'ctx')
The draws below stay inside these ranges and needn't reach their ends.
Inputs may be any that keep to these rules, and one draw needn't show every extreme that they name: `dest_replica`: every block of a pack receives exactly one arriving block; a block keeps its shard along ctx (dest_slot // 16 equals the arriving block's own b // 16); the 16 blocks of one device go to every pack, 1 to each. `dest_slot`: see dest_replica. `doc_lengths`: they sum to 256 in every pack, and the largest is 32 in every pack.
All inputs are finite; a program needn't handle non-finite values. No bound on the sum of `tile_mask` on one device may be relied on, other than what follows from the above.
Results may differ from the reference program's by a relative error of at most 0.0033.
Values may be sent and summed in bfloat16 or wider, within the bound.
A program may use at most 64 MiB of HBM per device.

```python
import math
import jax
import jax.numpy as jnp
import numpy as np
from jax import lax

HEAD_WIDTH = 128
QUERY_HEADS = 4
KEY_VALUE_HEADS = 1
TOK_DEV = 1024
BLK = 64
REACH = 2
PACK_COUNT = 16
PACK_TOKENS = 16384
NB_DEV = 16
CAP = 1
NBLK = 256
DOC_MOST = 32
DOCS = 64
N_CTX = 16


def routing_pair(key):
    column_total = NBLK // NB_DEV

    def one_column(column):
        column_key = jax.random.fold_in(jax.random.fold_in(key, 101), column)
        shifts = jax.random.permutation(jax.random.fold_in(column_key, 1), PACK_COUNT)[:NB_DEV // CAP]
        order_key = jax.random.fold_in(column_key, 2)

        def pack_ordering(pack):
            return jax.random.permutation(jax.random.fold_in(order_key, pack), NB_DEV).astype(jnp.int32)
        orderings = jax.vmap(pack_ordering)(jnp.arange(PACK_COUNT, dtype=jnp.int32))
        positions = jnp.arange(NB_DEV, dtype=jnp.int32)
        shift_of = shifts[positions // CAP].astype(jnp.int32)
        replicas = jnp.arange(PACK_COUNT, dtype=jnp.int32)
        target_replica = ((replicas[:, None] + shift_of[None, :]) % PACK_COUNT).astype(jnp.int32)
        chosen = jnp.take_along_axis(orderings, target_replica, axis=0).astype(jnp.int32)
        target_slot = (column * NB_DEV + chosen).astype(jnp.int32)
        return (target_replica, target_slot)
    target_replica, target_slot = jax.vmap(one_column)(jnp.arange(column_total, dtype=jnp.int32))
    target_replica = jnp.transpose(target_replica, (1, 0, 2)).reshape(PACK_COUNT, NBLK).astype(jnp.int32)
    target_slot = jnp.transpose(target_slot, (1, 0, 2)).reshape(PACK_COUNT, NBLK).astype(jnp.int32)
    return (target_replica, target_slot)


def draw_dest_replica(key, part):
    return routing_pair(key)[0]


def draw_dest_slot(key, part):
    return routing_pair(key)[1]


def query_key_pair(key):
    base_q = jax.random.normal(jax.random.fold_in(key, 201), (PACK_COUNT, PACK_TOKENS, QUERY_HEADS * HEAD_WIDTH), jnp.float32)
    starting_key = jax.random.normal(jax.random.fold_in(key, 202), (PACK_COUNT, PACK_TOKENS, KEY_VALUE_HEADS * HEAD_WIDTH), jnp.float32)
    return (jnp.clip(base_q, -6.0, 6.0), jnp.clip(starting_key, -6.0, 6.0))


def draw_queries(key, part):
    return query_key_pair(key)[0].astype(jnp.bfloat16)


def draw_keys(key, part):
    return query_key_pair(key)[1].astype(jnp.bfloat16)


def plant(values, key, low, high):
    index_at = [jax.random.randint(jax.random.fold_in(key, axis), (), 0, length) for axis, length in enumerate(values.shape)]
    widest = values.shape.index(max(values.shape))
    beside = index_at[:widest] + [(index_at[widest] + 1) % values.shape[widest]] + index_at[widest + 1:]
    return values.at[tuple(index_at)].set(low).at[tuple(beside)].set(high)


def level_of(stream_key, extent, split, least, top_value):
    factor_of = 1.0
    for position, parts in split:
        heights = jax.random.uniform(jax.random.fold_in(jax.random.fold_in(stream_key, 6), position), (parts,), jnp.float32, least / len(split), top_value / len(split))
        factor_of = factor_of * jnp.repeat(jnp.exp(heights), extent[position] // parts).reshape((-1,) + (1,) * (len(extent) - 1 - position))
    return factor_of


def profile(number_of, total, reach, skew):
    weights = [(1 << 20) // math.isqrt(grade ** skew) + 1 for grade in range(2, number_of + 1)]
    rest, counts = total - reach - (number_of - 1), [1] * (number_of - 1)
    while rest > 0:
        movable = [i for i in range(number_of - 1) if counts[i] < reach]
        pool, budget = sum([weights[i] for i in movable]), rest
        for i in movable:
            addition = min(reach - counts[i], max(1, budget * weights[i] // pool), rest)
            counts[i] = counts[i] + addition
            rest = rest - addition
    return np.array([reach] + counts)


def uneven(own_key, number_of, total, most, slope):
    if number_of == 2:
        one = jax.random.randint(own_key, (), max(1, total - most), min(most, total - 1) + 1)
        return jnp.stack([one, total - one])
    tallies = jnp.asarray(profile(number_of, total, most, slope), jnp.int32)
    pairs = (number_of - 1) // 2
    donor, receiver = tallies[1:1 + 2 * pairs:2], tallies[2:2 + 2 * pairs:2]
    room = jnp.minimum(donor - 1, most - receiver)
    moved = jax.random.randint(jax.random.fold_in(own_key, 1), (pairs,), 0, 1 << 20) % (room + 1)
    tallies = tallies.at[1:1 + 2 * pairs:2].set(donor - moved).at[2:2 + 2 * pairs:2].set(receiver + moved)
    return tallies[jax.random.permutation(jax.random.fold_in(own_key, 2), number_of)]


def noise(stream_key, shape, spread, limit, cuts=(), held_as=jnp.bfloat16):
    drawn = spread * jax.random.normal(stream_key, shape, jnp.float32)
    if cuts:
        drawn = drawn * level_of(stream_key, shape, cuts, -0.22, 0.18)
    return jnp.clip(drawn, -limit, limit).astype(held_as)


def setup_inputs(seed: int = 0) -> dict:
    key_of = jax.random.split(jax.random.key(seed), 8)
    return {
        "queries": draw_queries(jax.random.fold_in(key_of[7], 71), 0),
        "keys": draw_keys(jax.random.fold_in(key_of[7], 71), 0),
        "values": noise(key_of[2], (PACK_COUNT, PACK_TOKENS, KEY_VALUE_HEADS * HEAD_WIDTH), 1.0, 6.0, ((0, 16), (1, 16))),
        "dest_replica": draw_dest_replica(jax.random.fold_in(key_of[7], 71), 0),
        "dest_slot": draw_dest_slot(jax.random.fold_in(key_of[7], 71), 0),
        "doc_lengths": jax.vmap(lambda own: uneven(own, DOCS, NBLK, DOC_MOST, 2))(jax.random.split(key_of[5], PACK_COUNT)).reshape((PACK_COUNT, DOCS)).astype(jnp.int32),
        "tile_mask": plant((jax.random.randint(key_of[6], (PACK_COUNT, NBLK, NBLK), 0, 4) < 3).astype(jnp.int32), jax.random.fold_in(key_of[6], 1), 0, 1),
    }


def block_docs(ends, block_ids):
    return jnp.sum((ends[None, :] <= block_ids[:, None]).astype(jnp.int32), axis=1).astype(jnp.int32)


def shard_attend(rows_of_queries, rows_of_keys, rows_of_values, allowed):
    count_of_rows = rows_of_queries.shape[0]
    query_group_width = QUERY_HEADS // KEY_VALUE_HEADS
    heads_of_queries = rows_of_queries.astype(jnp.float32).reshape(count_of_rows, KEY_VALUE_HEADS, query_group_width, HEAD_WIDTH)
    heads_of_keys = rows_of_keys.astype(jnp.float32).reshape(count_of_rows, KEY_VALUE_HEADS, HEAD_WIDTH)
    heads_of_values = rows_of_values.astype(jnp.float32).reshape(count_of_rows, KEY_VALUE_HEADS, HEAD_WIDTH)
    scores = jnp.einsum("qhgd,khd->hgqk", heads_of_queries, heads_of_keys) * (HEAD_WIDTH ** -0.5)
    masked = jnp.where(allowed, scores, -jnp.inf)
    row_max = jnp.max(masked, axis=-1)
    present = jnp.any(allowed, axis=-1)
    safe_max = jnp.where(present, row_max, jnp.float32(0.0))
    weights = jnp.where(allowed, jnp.exp(scores - safe_max[..., None]), jnp.float32(0.0))
    row_sum = jnp.sum(weights, axis=-1)
    rounded = lax.optimization_barrier(weights.astype(jnp.bfloat16))
    partial_value = jnp.einsum("hgqk,khd->qhgd", rounded.astype(jnp.float32), heads_of_values)
    return row_max, row_sum, partial_value


def combine(portions):
    overall = portions[0][0]
    for portion in portions[1:]:
        overall = jnp.maximum(overall, portion[0])
    denominator = jnp.zeros_like(overall)
    numerator = jnp.zeros_like(portions[0][2])
    for portion in portions:
        factor = jnp.exp(portion[0] - overall)
        denominator = denominator + factor * portion[1]
        numerator = numerator + jnp.transpose(factor, (2, 0, 1))[..., None] * portion[2]
    result = numerator / jnp.transpose(denominator, (2, 0, 1))[..., None]
    return result.reshape(result.shape[0], -1).astype(jnp.bfloat16)


def reference(queries, keys, values, dest_replica, dest_slot, doc_lengths, tile_mask):
    targets = (dest_replica * NBLK + dest_slot).reshape(-1).astype(jnp.int32)

    def route(array):
        blocks = array.reshape(PACK_COUNT * NBLK, BLK, array.shape[-1])
        placed = jnp.zeros_like(blocks).at[targets].set(blocks)
        return placed.reshape(PACK_COUNT, PACK_TOKENS, array.shape[-1])

    routed_q = route(queries)
    routed_k = route(keys)
    routed_v = route(values)
    ends = jnp.cumsum(doc_lengths, axis=1).astype(jnp.int32)
    block_index = jnp.arange(NB_DEV, dtype=jnp.int32)
    token_index = jnp.arange(TOK_DEV, dtype=jnp.int32)

    def one_shard(index):
        replica = (index // N_CTX).astype(jnp.int32)
        column = (index % N_CTX).astype(jnp.int32)
        pack_q = lax.dynamic_index_in_dim(routed_q, replica, 0, keepdims=False)
        pack_k = lax.dynamic_index_in_dim(routed_k, replica, 0, keepdims=False)
        pack_v = lax.dynamic_index_in_dim(routed_v, replica, 0, keepdims=False)
        pack_ends = lax.dynamic_index_in_dim(ends, replica, 0, keepdims=False)
        pack_mask = lax.dynamic_index_in_dim(tile_mask, replica, 0, keepdims=False)
        mask_rows = lax.dynamic_slice_in_dim(pack_mask, (column * NB_DEV).astype(jnp.int32), NB_DEV, 0)
        rows_of_queries = lax.dynamic_slice_in_dim(pack_q, (column * TOK_DEV).astype(jnp.int32), TOK_DEV, 0)
        query_blocks = column * NB_DEV + block_index
        query_docs = block_docs(pack_ends, query_blocks)
        query_pos = column * TOK_DEV + token_index
        portions = []
        for offset in range(REACH + 1):
            source = jnp.maximum(column - offset, 0).astype(jnp.int32)
            rows_of_keys = lax.dynamic_slice_in_dim(pack_k, (source * TOK_DEV).astype(jnp.int32), TOK_DEV, 0)
            rows_of_values = lax.dynamic_slice_in_dim(pack_v, (source * TOK_DEV).astype(jnp.int32), TOK_DEV, 0)
            key_blocks = (column - offset) * NB_DEV + block_index
            key_docs = block_docs(pack_ends, key_blocks)
            mask_cols = lax.dynamic_slice_in_dim(mask_rows, (source * NB_DEV).astype(jnp.int32), NB_DEV, 1)
            tile_ok = (query_docs[:, None] == key_docs[None, :]) & (key_blocks[None, :] <= query_blocks[:, None])
            tile_ok = tile_ok & ((mask_cols == 1) | (key_blocks[None, :] == query_blocks[:, None]))
            tile_ok = tile_ok & (key_blocks[None, :] >= 0)
            expanded = jnp.repeat(jnp.repeat(tile_ok, BLK, axis=0), BLK, axis=1)
            key_pos = (column - offset) * TOK_DEV + token_index
            allowed = expanded & (key_pos[None, :] <= query_pos[:, None])
            portions.append(shard_attend(rows_of_queries, rows_of_keys, rows_of_values, allowed))
        return combine(portions)

    shards = lax.map(one_shard, jnp.arange(PACK_COUNT * N_CTX, dtype=jnp.int32))
    return shards.reshape(PACK_COUNT, PACK_TOKENS, QUERY_HEADS * HEAD_WIDTH)
```

```python
import functools

import jax
import jax.numpy as jnp
from jax import lax
from jax.experimental import pallas as pl
from jax.experimental.pallas import tpu as pltpu
from jax.sharding import PartitionSpec as P

MESH = pl.DeviceIdType.MESH
HEADS = 4
WIDTH = 128
BLK = 64
NB = 16
TOK = NB * BLK
ROWS = HEADS * BLK
KEYS = 256
SCALE = WIDTH ** (-0.5) * 1.4426950408889634
LOW = -32768.0
CHUNKS = 4
PER = NB // CHUNKS


def tile_bias(col, docs_ref, mask_ref):
    count = docs_ref.shape[1]
    blocks = mask_ref.shape[1]
    lengths = docs_ref[...].astype(jnp.float32)
    upto = lax.broadcasted_iota(jnp.int32, (count, count), 1) <= lax.broadcasted_iota(jnp.int32, (count, count), 0)
    ends = jnp.sum(jnp.where(upto, jnp.broadcast_to(lengths, (count, count)), 0.0), axis=1, keepdims=True)
    block = lax.broadcasted_iota(jnp.int32, (count, blocks), 1).astype(jnp.float32)
    key_doc = jnp.sum(jnp.where(ends <= block, 1.0, 0.0), axis=0, keepdims=True)
    key_doc = jnp.broadcast_to(key_doc, (NB, blocks))
    key_block = lax.broadcasted_iota(jnp.int32, (NB, blocks), 1)
    query_block = lax.broadcasted_iota(jnp.int32, (NB, blocks), 0) + col * NB
    own = key_block == query_block
    query_doc = jnp.sum(jnp.where(own, key_doc, 0.0), axis=1, keepdims=True)
    ok = (key_doc == query_doc) & (key_block <= query_block) & ((mask_ref[...] == 1) | own)
    ok = jnp.where(ok, 1.0, 0.0).astype(jnp.bfloat16)
    window = lax.broadcasted_iota(jnp.int32, (blocks, 128), 1) + (col - 2) * NB
    pick = jnp.where(lax.broadcasted_iota(jnp.int32, (blocks, 128), 0) == window, 1.0, 0.0).astype(jnp.bfloat16)
    ok = jnp.dot(ok, pick, preferred_element_type=jnp.float32)
    return ((1.0 - ok) * LOW).astype(jnp.bfloat16)


def kernel(
    n, columns, q_ref, k_ref, v_ref, rep_ref, rep_vec, slot_vec, docs_ref, mask_ref, out_ref,
    kv_send, kv_recv, q_send, q_recv, code_send, code_recv, halo, q_aug, k_aug, v_aug, bias, acc, top, src,
    kv_sent, kv_got, q_sent, q_got, code_sent, code_got, halo_sent, halo_got,
):
    me = lax.axis_index("dp")
    col = lax.axis_index("ctx")
    right = lax.rem(col + 1, columns)
    left = lax.rem(col + columns - 1, columns)

    barrier = pltpu.get_barrier_semaphore()

    def greet(d, carry):
        pl.semaphore_signal(barrier, inc=1, device_id={"dp": lax.rem(me + d, n)}, device_id_type=MESH)
        return carry

    lax.fori_loop(1, n, greet, 0)
    pl.semaphore_signal(barrier, inc=1, device_id={"ctx": right}, device_id_type=MESH)
    pl.semaphore_signal(barrier, inc=1, device_id={"ctx": left}, device_id_type=MESH)

    code_send[...] = jnp.full((1, 128), -1, jnp.int32)
    code_send[:, :NB] = rep_vec[...] * NB + slot_vec[...] - col * NB

    def block_for(peer):
        where = jnp.int32(0)
        for j in range(NB):
            where = jnp.where(rep_ref[0, j] == peer, j, where)
        return where

    def pack_kv(peer, carry):
        j = block_for(peer)
        kv_send[peer, 0] = k_ref[j]
        kv_send[peer, 1] = v_ref[j]
        return carry

    lax.fori_loop(0, n, pack_kv, 0)

    def kv_copy(peer, slot):
        return pltpu.make_async_remote_copy(
            src_ref=kv_send.at[peer], dst_ref=kv_recv.at[slot], send_sem=kv_sent.at[peer],
            recv_sem=kv_got.at[slot], device_id={"dp": peer}, device_id_type=MESH)

    def q_copy(peer, slot):
        return pltpu.make_async_remote_copy(
            src_ref=q_send.at[peer], dst_ref=q_recv.at[slot], send_sem=q_sent.at[peer],
            recv_sem=q_got.at[slot], device_id={"dp": peer}, device_id_type=MESH)

    def code_copy(peer, slot):
        return pltpu.make_async_remote_copy(
            src_ref=code_send, dst_ref=code_recv.at[slot], send_sem=code_sent.at[peer],
            recv_sem=code_got.at[slot], device_id={"dp": peer}, device_id_type=MESH)

    pl.semaphore_wait(barrier, n + 1)

    def send_kv(d, carry):
        peer = lax.rem(me + d, n)
        code_copy(peer, me).start()
        kv_copy(peer, me).start()
        return carry

    lax.fori_loop(1, n, send_kv, 0)

    def send_q(d, carry):
        peer = lax.rem(me + d, n)
        q_send[peer] = q_ref[block_for(peer)]
        q_copy(peer, me).start()
        return carry

    lax.fori_loop(1, n, send_q, 0)
    mine = block_for(me)
    q_recv[me] = q_ref[mine]
    kv_recv[me, 0] = k_ref[mine]
    kv_recv[me, 1] = v_ref[mine]
    code_recv[me] = code_send[...]

    rows = tile_bias(col, docs_ref, mask_ref).astype(jnp.float32)
    for i in range(NB):
        bias[i] = jnp.broadcast_to(rows[i:i + 1], (16, 128)).astype(jnp.bfloat16)
    key_at = lax.broadcasted_iota(jnp.int32, (TOK, 128), 0) // BLK
    lane = lax.broadcasted_iota(jnp.int32, (TOK, 128), 1)
    for p in range(3):
        k_aug[p, :, WIDTH:] = jnp.where(lane == key_at + (2 - p) * NB, 1.0, 0.0).astype(jnp.bfloat16)
        v_aug[p, :, WIDTH:] = jnp.ones((TOK, 128), jnp.bfloat16)

    def got_kv(d, carry):
        peer = lax.rem(me + n - d, n)
        code_copy(peer, peer).wait_recv()
        kv_copy(peer, peer).wait_recv()
        return carry

    lax.fori_loop(1, n, got_kv, 0)
    codes = code_recv[...].reshape(n, 128)
    sender = lax.broadcasted_iota(jnp.int32, (n, 128), 0)
    for i in range(NB):
        src[i] = jnp.max(jnp.where(codes == me * NB + i, sender, 0))

    def place_kv(i, carry):
        s = src[i]
        rows = pl.ds(pl.multiple_of(i * BLK, BLK), BLK)
        key, value = kv_recv[s, 0], kv_recv[s, 1]
        halo[0, i, 0] = key
        halo[0, i, 1] = value
        k_aug[0, rows, :WIDTH] = key
        v_aug[0, rows, :WIDTH] = value
        return carry

    lax.fori_loop(0, NB, place_kv, 0)

    def halo_copy(hop, chunk):
        part = pl.ds(chunk * PER, PER)
        return pltpu.make_async_remote_copy(
            src_ref=halo.at[hop, part], dst_ref=halo.at[hop + 1, part], send_sem=halo_sent.at[hop, chunk],
            recv_sem=halo_got.at[hop, chunk], device_id={"ctx": right}, device_id_type=MESH)

    for chunk in range(CHUNKS):
        halo_copy(0, chunk).start()

    def got_q(d, carry):
        peer = lax.rem(me + n - d, n)
        q_copy(peer, peer).wait_recv()
        return carry

    lax.fori_loop(1, n, got_q, 0)

    def attend(i, p, lo, hi, diag=None):
        if p == 0:
            block = q_recv[src[i]]
            heads = jnp.concatenate([block[:, h * WIDTH:(h + 1) * WIDTH] for h in range(HEADS)], axis=0)
            query = jnp.concatenate([heads, jnp.concatenate([bias[i]] * (ROWS // 16), axis=0)], axis=1)
            q_aug[i] = query
        else:
            query = q_aug[i]
        score = lax.dot_general(
            query, k_aug[p, lo:hi, :], (((1,), (1,)), ((), ())), preferred_element_type=jnp.float32)
        if diag is not None:
            at = lax.rem(lax.broadcasted_iota(jnp.int32, (ROWS, KEYS), 0), BLK) + diag * BLK
            last = jnp.where(lax.broadcasted_iota(jnp.int32, (ROWS, KEYS), 1) <= at, score[:, -KEYS:], LOW)
            score = last if hi - lo == KEYS else jnp.concatenate([score[:, :-KEYS], last], axis=1)
        high = jnp.broadcast_to(jnp.max(score, axis=1, keepdims=True), (ROWS, 128))
        if p > 0:
            before = top[i]
            high = jnp.maximum(high, before)
        weight = jnp.exp2((score - jnp.concatenate([high] * ((hi - lo) // 128), axis=1)) * SCALE)
        part = jnp.dot(weight.astype(jnp.bfloat16), v_aug[p, lo:hi, :], preferred_element_type=jnp.float32)
        if p > 0:
            factor = jnp.exp2((before - high) * SCALE)
            part = part + acc[i] * jnp.concatenate([factor, factor], axis=1)
        if p < 2:
            acc[i] = part
            top[i] = high
        else:
            result = (part[:, :WIDTH] / part[:, WIDTH:]).astype(jnp.bfloat16)
            for h in range(HEADS):
                out_ref[i, :, h * WIDTH:(h + 1) * WIDTH] = result[h * BLK:(h + 1) * BLK]

    def sweep(p, first, count, lo, hi, diag=False):
        def step(j, carry):
            attend(first + j, p, lo, hi, j if diag else None)
            return carry

        lax.fori_loop(0, count, step, 0)

    def take_halo(hop):
        def place(i, carry):
            rows = pl.ds(pl.multiple_of(i * BLK, BLK), BLK)
            k_aug[hop, rows, :WIDTH] = halo[hop, i, 0]
            v_aug[hop, rows, :WIDTH] = halo[hop, i, 1]
            return carry

        lax.fori_loop(0, NB, place, 0)

    for g in range(4):
        sweep(0, g * 4, 4, 0, (g + 1) * KEYS, True)
        halo_copy(0, g).wait_recv()
        halo_copy(1, g).start()
    take_halo(1)
    sweep(1, 0, NB, 0, TOK)
    for chunk in range(CHUNKS):
        halo_copy(1, chunk).wait_recv()
    take_halo(2)
    sweep(2, 0, 3, 0, TOK)
    sweep(2, 3, 4, KEYS, TOK)
    sweep(2, 7, 4, 2 * KEYS, TOK)
    sweep(2, 11, 5, 3 * KEYS, TOK)

    for chunk in range(CHUNKS):
        halo_copy(0, chunk).wait_send()
        halo_copy(1, chunk).wait_send()

    def sent(d, carry):
        peer = lax.rem(me + d, n)
        code_copy(peer, me).wait_send()
        kv_copy(peer, me).wait_send()
        q_copy(peer, me).wait_send()
        return carry

    lax.fori_loop(1, n, sent, 0)


def per_device(n, columns, queries, keys, values, dest_replica, dest_slot, doc_lengths, tile_mask):
    q = queries.reshape(NB, BLK, HEADS * WIDTH)
    k = keys.reshape(NB, BLK, WIDTH)
    v = values.reshape(NB, BLK, WIDTH)
    vmem = pl.BlockSpec(memory_space=pltpu.VMEM)
    smem = pl.BlockSpec(memory_space=pltpu.SMEM)
    bf16, f32, i32 = jnp.bfloat16, jnp.float32, jnp.int32
    dma = pltpu.SemaphoreType.DMA
    out = pl.pallas_call(
        functools.partial(kernel, n, columns),
        out_shape=jax.ShapeDtypeStruct((NB, BLK, HEADS * WIDTH), bf16),
        in_specs=[vmem, vmem, vmem, smem, vmem, vmem, vmem, vmem],
        out_specs=vmem,
        scratch_shapes=[
            pltpu.VMEM((n, 2, BLK, WIDTH), bf16),
            pltpu.VMEM((n, 2, BLK, WIDTH), bf16),
            pltpu.VMEM((n, BLK, HEADS * WIDTH), bf16),
            pltpu.VMEM((n, BLK, HEADS * WIDTH), bf16),
            pltpu.VMEM((1, 128), i32),
            pltpu.VMEM((n, 1, 128), i32),
            pltpu.VMEM((3, NB, 2, BLK, WIDTH), bf16),
            pltpu.VMEM((NB, ROWS, 2 * WIDTH), bf16),
            pltpu.VMEM((3, TOK, 2 * WIDTH), bf16),
            pltpu.VMEM((3, TOK, 2 * WIDTH), bf16),
            pltpu.VMEM((NB, 16, 128), bf16),
            pltpu.VMEM((NB, ROWS, 2 * WIDTH), f32),
            pltpu.VMEM((NB, ROWS, 128), f32),
            pltpu.SMEM((NB,), i32),
            dma((n,)), dma((n,)), dma((n,)), dma((n,)), dma((n,)), dma((n,)),
            dma((2, CHUNKS)), dma((2, CHUNKS)),
        ],
        compiler_params=pltpu.CompilerParams(
            collective_id=0, has_side_effects=True, vmem_limit_bytes=48 * 1024 * 1024),
        cost_estimate=pl.CostEstimate(flops=10**10, bytes_accessed=4 * 2**20, transcendentals=10**7),
    )(q, k, v, dest_replica, dest_replica, dest_slot, doc_lengths, tile_mask[0])
    return out.reshape(1, TOK, HEADS * WIDTH)


def solution(mesh):
    n, columns = mesh.shape["dp"], mesh.shape["ctx"]
    return jax.shard_map(
        functools.partial(per_device, n, columns),
        mesh=mesh,
        in_specs=(
            P("dp", "ctx", None),
            P("dp", "ctx", None),
            P("dp", "ctx", None),
            P("dp", "ctx"),
            P("dp", "ctx"),
            P("dp", None),
            P("dp", "ctx", None),
        ),
        out_specs=P("dp", "ctx", None),
        check_vma=False,
    )
```

```python
import functools

import jax
import jax.numpy as jnp
from jax import lax
from jax.experimental import pallas as pl
from jax.experimental.pallas import tpu as pltpu
from jax.sharding import PartitionSpec as P

MESH = pl.DeviceIdType.MESH
HEADS = 4
WIDTH = 128
BLK = 64
NB = 16
TOK = NB * BLK
ROWS = HEADS * BLK
KEYS = 256
SCALE = WIDTH ** (-0.5) * 1.4426950408889634
LOW = -32768.0
CHUNKS = 4
PER = NB // CHUNKS
PAIR = 2
GROUP = PAIR * ROWS
ORDER = (3, 2, 1, 0)
DETOUR = (2, 0)


def tile_bias(col, docs_ref, mask_ref):
    count = docs_ref.shape[1]
    blocks = mask_ref.shape[1]
    lengths = docs_ref[...].astype(jnp.float32)
    upto = lax.broadcasted_iota(jnp.int32, (count, count), 1) <= lax.broadcasted_iota(jnp.int32, (count, count), 0)
    ends = jnp.sum(jnp.where(upto, jnp.broadcast_to(lengths, (count, count)), 0.0), axis=1, keepdims=True)
    block = lax.broadcasted_iota(jnp.int32, (count, blocks), 1).astype(jnp.float32)
    key_doc = jnp.sum(jnp.where(ends <= block, 1.0, 0.0), axis=0, keepdims=True)
    key_doc = jnp.broadcast_to(key_doc, (NB, blocks))
    key_block = lax.broadcasted_iota(jnp.int32, (NB, blocks), 1)
    query_block = lax.broadcasted_iota(jnp.int32, (NB, blocks), 0) + col * NB
    own = key_block == query_block
    query_doc = jnp.sum(jnp.where(own, key_doc, 0.0), axis=1, keepdims=True)
    ok = (key_doc == query_doc) & (key_block <= query_block) & ((mask_ref[...] == 1) | own)
    ok = jnp.where(ok, 1.0, 0.0).astype(jnp.bfloat16)
    window = lax.broadcasted_iota(jnp.int32, (blocks, 128), 1) + (col - 2) * NB
    pick = jnp.where(lax.broadcasted_iota(jnp.int32, (blocks, 128), 0) == window, 1.0, 0.0).astype(jnp.bfloat16)
    ok = jnp.dot(ok, pick, preferred_element_type=jnp.float32)
    return ((1.0 - ok) * LOW).astype(jnp.bfloat16)


def kernel(
    n, columns, q_hbm, k_hbm, v_hbm, rep_hbm, slot_hbm, docs_hbm, mask_hbm, out_ref,
    q_ref, k_ref, v_ref, rep_ref, rep_vec, slot_vec, docs_ref, mask_ref, load_sem,
    kv_send, kv_recv, q_send, q_recv, code_send, code_recv, halo, relay, q_aug, k_aug, v_aug, bias, acc, top, acc_tail, top_tail, src, at, slot_of,
    score_a, high_a, score_b, high_b,
    kv_sent, kv_got, q_sent, q_got, code_sent, code_got, halo_sent, halo_got,
    detour_sent, detour_got, relay_sent,
):
    me = lax.axis_index("dp")
    col = lax.axis_index("ctx")
    last = columns - 1
    bend = columns // 2 - 1
    right = lax.rem(col + 1, columns)
    left = lax.rem(col + columns - 1, columns)

    loads = [
        pltpu.make_async_copy(a, b, load_sem.at[i])
        for i, (a, b) in enumerate((
            (rep_hbm, rep_ref), (rep_hbm, rep_vec), (slot_hbm, slot_vec), (k_hbm, k_ref), (v_hbm, v_ref),
            (q_hbm, q_ref), (docs_hbm, docs_ref), (mask_hbm, mask_ref)))
    ]
    for load in loads:
        load.start()

    barrier = pltpu.get_barrier_semaphore()

    def greet(d, carry):
        pl.semaphore_signal(barrier, inc=1, device_id={"dp": lax.rem(me + d, n)}, device_id_type=MESH)
        return carry

    lax.fori_loop(1, n, greet, 0)

    @pl.when(col > 0)
    def _():
        pl.semaphore_signal(barrier, inc=1, device_id={"ctx": left}, device_id_type=MESH)

    @pl.when(col == last)
    def _():
        pl.semaphore_signal(barrier, inc=1, device_id={"ctx": bend}, device_id_type=MESH)

    @pl.when(col == bend + 1)
    def _():
        pl.semaphore_signal(barrier, inc=1, device_id={"ctx": last}, device_id_type=MESH)

    for load in loads[:5]:
        load.wait()
    code_send[...] = jnp.full((1, 128), -1, jnp.int32)
    code_send[:, :NB] = rep_vec[...] * NB + slot_vec[...] - col * NB

    def block_for(peer):
        where = jnp.int32(0)
        for j in range(NB):
            where = jnp.where(rep_ref[0, j] == peer, j, where)
        return where

    def pack_kv(peer, carry):
        j = block_for(peer)
        kv_send[peer, 0] = k_ref[j]
        kv_send[peer, 1] = v_ref[j]
        return carry

    lax.fori_loop(0, n, pack_kv, 0)

    def kv_copy(peer, slot):
        return pltpu.make_async_remote_copy(
            src_ref=kv_send.at[peer], dst_ref=kv_recv.at[slot], send_sem=kv_sent.at[peer],
            recv_sem=kv_got.at[slot], device_id={"dp": peer}, device_id_type=MESH)

    def q_copy(peer, slot):
        return pltpu.make_async_remote_copy(
            src_ref=q_send.at[peer], dst_ref=q_recv.at[slot], send_sem=q_sent.at[peer],
            recv_sem=q_got.at[slot], device_id={"dp": peer}, device_id_type=MESH)

    def code_copy(peer, slot):
        return pltpu.make_async_remote_copy(
            src_ref=code_send, dst_ref=code_recv.at[slot], send_sem=code_sent.at[peer],
            recv_sem=code_got.at[slot], device_id={"dp": peer}, device_id_type=MESH)

    pl.semaphore_wait(barrier, n + jnp.where(col == bend, 1, 0))

    def send_kv(d, carry):
        peer = lax.rem(me + d, n)
        code_copy(peer, me).start()
        kv_copy(peer, me).start()
        return carry

    lax.fori_loop(1, n, send_kv, 0)
    loads[5].wait()

    def send_q(d, carry):
        peer = lax.rem(me + d, n)
        q_send[peer] = q_ref[block_for(peer)]
        q_copy(peer, me).start()
        return carry

    lax.fori_loop(1, n, send_q, 0)
    mine = block_for(me)
    q_recv[me] = q_ref[mine]
    kv_recv[me, 0] = k_ref[mine]
    kv_recv[me, 1] = v_ref[mine]
    code_recv[me] = code_send[...]

    loads[6].wait()
    loads[7].wait()
    rows = tile_bias(col, docs_ref, mask_ref).astype(jnp.float32)
    for i in range(NB):
        bias[i] = jnp.broadcast_to(rows[i:i + 1], (16, 128)).astype(jnp.bfloat16)
    key_at = lax.broadcasted_iota(jnp.int32, (TOK, 128), 0) // BLK
    lane = lax.broadcasted_iota(jnp.int32, (TOK, 128), 1)
    for p in range(3):
        k_aug[p, :, WIDTH:] = jnp.where(lane == key_at + (2 - p) * NB, 1.0, 0.0).astype(jnp.bfloat16)
        v_aug[p, :, WIDTH:] = jnp.ones((TOK, 128), jnp.bfloat16)
    nothing = jnp.zeros((2, BLK, WIDTH), jnp.bfloat16)
    halo[2, 0] = nothing
    for hop in (1, 2):
        @pl.when(col < hop)
        def _():
            for i in range(NB):
                halo[hop, i] = nothing

    def got_code(d, carry):
        peer = lax.rem(me + n - d, n)
        code_copy(peer, peer).wait_recv()
        return carry

    lax.fori_loop(1, n, got_code, 0)
    codes = code_recv[...].reshape(n, 128)
    sender = lax.broadcasted_iota(jnp.int32, (n, 128), 0)
    for i in range(NB):
        source = jnp.max(jnp.where(codes == me * NB + i, sender, 0))
        src[i] = source
        at[i] = lax.rem(me - source + n, n)
    for d in range(n):
        row = code_recv[lax.rem(me - d + n, n)]
        slot_of[d] = jnp.max(jnp.where((row >= me * NB) & (row < (me + 1) * NB), row - me * NB, 0))

    def got_kv(d, carry):
        peer = lax.rem(me + n - d, n)
        kv_copy(peer, peer).wait_recv()
        return carry

    lax.fori_loop(1, n, got_kv, 0)

    def part_of(hop, chunk):
        return pl.ds(1, PER - 1) if hop == 1 and chunk == 0 else pl.ds(chunk * PER, PER)

    def halo_copy(hop, chunk):
        part = part_of(hop, chunk)
        return pltpu.make_async_remote_copy(
            src_ref=halo.at[hop, part], dst_ref=halo.at[hop + 1, part], send_sem=halo_sent.at[hop, chunk],
            recv_sem=halo_got.at[hop, chunk], device_id={"ctx": right}, device_id_type=MESH)

    def detour_copy(hop, chunk):
        part = part_of(hop, chunk)
        return pltpu.make_async_remote_copy(
            src_ref=halo.at[hop, part], dst_ref=relay.at[hop, part], send_sem=detour_sent.at[hop, chunk],
            recv_sem=detour_got.at[hop, chunk], device_id={"ctx": last}, device_id_type=MESH)

    def relay_copy(hop, chunk):
        part = part_of(hop, chunk)
        return pltpu.make_async_remote_copy(
            src_ref=relay.at[hop, part], dst_ref=halo.at[hop + 1, part], send_sem=relay_sent.at[hop, chunk],
            recv_sem=halo_got.at[hop, chunk], device_id={"ctx": bend + 1}, device_id_type=MESH)

    def send_halo(hop, chunk):
        first = col >= hop
        if chunk in DETOUR:
            @pl.when(first & (col < last) & (col != bend))
            def _():
                halo_copy(hop, chunk).start()

            @pl.when(col == bend)
            def _():
                detour_copy(hop, chunk).start()
        else:
            @pl.when(first & (col < last))
            def _():
                halo_copy(hop, chunk).start()

    def pass_on(hop, chunk):
        @pl.when(col == last)
        def _():
            detour_copy(hop, chunk).wait_recv()
            relay_copy(hop, chunk).start()

    def got_halo(hop, chunk):
        @pl.when(col > hop)
        def _():
            halo_copy(hop, chunk).wait_recv()

    def forward(chunk):
        got_halo(0, chunk)
        send_halo(1, chunk)

    def place_kv(i, carry):
        s = src[i]
        rows = pl.ds(pl.multiple_of(i * BLK, BLK), BLK)
        key, value = kv_recv[s, 0], kv_recv[s, 1]
        halo[0, i, 0] = key
        halo[0, i, 1] = value
        k_aug[0, rows, :WIDTH] = key
        v_aug[0, rows, :WIDTH] = value
        return carry

    for chunk in ORDER:
        lax.fori_loop(chunk * PER, (chunk + 1) * PER, place_kv, 0)
        send_halo(0, chunk)

    def got_q(d):
        peer = lax.rem(me + n - d, n)
        q_copy(peer, peer).wait_recv()

    def wide(value, width):
        return jnp.concatenate([value] * (width // 128), axis=1)

    def score(p, i, lo, hi, buffer, high):
        if p == 0:
            parts = []
            for b in range(PAIR):
                block = q_recv[lax.rem(me - (i + b) + n, n)]
                rows = bias[slot_of[i + b]]
                heads = jnp.concatenate([block[:, h * WIDTH:(h + 1) * WIDTH] for h in range(HEADS)], axis=0)
                part = jnp.concatenate([heads, jnp.concatenate([rows] * (ROWS // 16), axis=0)], axis=1)
                q_aug[i + b] = part
                parts.append(part)
            query = jnp.concatenate(parts, axis=0)
        elif p == 1:
            query = q_aug[pl.ds(i, PAIR)].reshape(GROUP, 2 * WIDTH)
        else:
            query = jnp.concatenate([q_aug[at[i + b]] for b in range(PAIR)], axis=0)
        width = hi - lo
        value = lax.dot_general(
            query, k_aug[min(p, 2), lo:hi, :], (((1,), (1,)), ((), ())), preferred_element_type=jnp.float32)
        if p == 0:
            row = lax.broadcasted_iota(jnp.int32, (GROUP, 128), 0)
            upto = lax.rem(row, BLK) + jnp.where(row < ROWS, slot_of[i], slot_of[i + 1]) * BLK
            key = lax.broadcasted_iota(jnp.int32, (GROUP, TOK), 1)
            value = jnp.where(key <= wide(upto, TOK), value, LOW)
        buffer[:, :width] = value
        most = value[:, :128]
        for c in range(128, width, 128):
            most = jnp.maximum(most, value[:, c:c + 128])
        high[...] = jnp.broadcast_to(jnp.max(most, axis=1, keepdims=True), (GROUP, 128))

    def soft(p, i, lo, hi, buffer, high):
        width = hi - lo
        most = high[...]
        total = None
        if p == 1:
            before = top[pl.ds(i, PAIR)].reshape(GROUP, 128)
            total = acc[pl.ds(i, PAIR)].reshape(GROUP, 2 * WIDTH)
        elif p in (2, 3):
            before = jnp.concatenate([top[at[i + b]] for b in range(PAIR)], axis=0)
            total = jnp.concatenate([acc[at[i + b]] for b in range(PAIR)], axis=0)
        elif p == 4:
            before = top_tail[pl.ds(i, PAIR)].reshape(GROUP, 128)
            total = acc_tail[pl.ds(i, PAIR)].reshape(GROUP, 2 * WIDTH)
        if total is not None:
            most = jnp.maximum(most, before)
        weight = jnp.exp2((buffer[:, :width] - wide(most, width)) * SCALE)
        part = jnp.dot(
            weight.astype(jnp.bfloat16), v_aug[min(p, 2), lo:hi, :], preferred_element_type=jnp.float32)
        if total is not None:
            factor = jnp.exp2((before - most) * SCALE)
            part = part + total * wide(factor, 2 * WIDTH)
        if p < 2:
            acc[pl.ds(i, PAIR)] = part.reshape(PAIR, ROWS, 2 * WIDTH)
            top[pl.ds(i, PAIR)] = most.reshape(PAIR, ROWS, 128)
        elif p == 3:
            acc_tail[pl.ds(i, PAIR)] = part.reshape(PAIR, ROWS, 2 * WIDTH)
            top_tail[pl.ds(i, PAIR)] = most.reshape(PAIR, ROWS, 128)
        else:
            result = (part[:, :WIDTH] / part[:, WIDTH:]).astype(jnp.bfloat16)
            for b in range(PAIR):
                for h in range(HEADS):
                    first = b * ROWS + h * BLK
                    out_ref[i + b, :, h * WIDTH:(h + 1) * WIDTH] = result[first:first + BLK]

    def take_halo(hop, chunk):
        for i in range(chunk * PER, (chunk + 1) * PER):
            k_aug[hop, i * BLK:(i + 1) * BLK, :WIDTH] = halo[hop, i, 0]
            v_aug[hop, i * BLK:(i + 1) * BLK, :WIDTH] = halo[hop, i, 1]

    def second(chunk):
        got_halo(1, chunk)
        take_halo(2, chunk)

    def arrive():
        for chunk in ORDER:
            take_halo(1, chunk)

    steps = [(0, i, 0, TOK) for i in range(0, NB, PAIR)]
    count = len(steps)
    steps += [(1, i, 0, TOK) for i in range(0, NB, PAIR)]
    steps += [(2, i, min((i + 1) // PER, 3) * KEYS, TOK) for i in range(NB - PAIR, PER - 1, -PAIR)]
    steps += [(3, i, KEYS, TOK) for i in range(PER - PAIR, -1, -PAIR)]
    final = len(steps)
    steps += [(4, i, 0, KEYS) for i in range(PER - PAIR, -1, -PAIR)]
    before = {k: [] for k in range(len(steps))}
    for k in range(count):
        for b in range(PAIR):
            if k * PAIR + b:
                before[k].append(functools.partial(got_q, k * PAIR + b))
    before[2] += [lambda: pass_on(0, 2), lambda: forward(3)]
    before[4] += [lambda: forward(2)]
    before[5] += [lambda: pass_on(0, 0)]
    before[6] += [lambda: forward(1)]
    before[7] += [lambda: pass_on(1, 2)]
    before[count] += [lambda: forward(0), arrive]
    before[count + 1] += [lambda: pass_on(1, 0)]
    before[2 * count] += [lambda: second(3)]
    before[2 * count + 2] += [lambda: second(2)]
    before[2 * count + 4] += [lambda: second(1)]
    before[final] += [lambda: second(0)]
    buffers = ((score_a, high_a), (score_b, high_b))
    for act in before[0]:
        act()
    score(*steps[0], *buffers[0])
    k = 0
    while k < len(steps):
        for act in before.get(k + 1, ()):
            act()
        if k == count:
            def two(j, carry):
                for u in range(2):
                    i = (2 * j + u) * PAIR
                    score(1, i + PAIR, 0, TOK, *buffers[(u + 1) % 2])
                    soft(1, i, 0, TOK, *buffers[u])
                return carry

            lax.fori_loop(0, count // 2 - 1, two, 0)
            k = 2 * count - 2
        if k + 1 < len(steps):
            score(*steps[k + 1], *buffers[(k + 1) % 2])
        soft(*steps[k], *buffers[k % 2])
        k += 1

    for hop in range(2):
        for chunk in range(CHUNKS):
            first = col >= hop
            if chunk in DETOUR:
                @pl.when(first & (col < last) & (col != bend))
                def _():
                    halo_copy(hop, chunk).wait_send()

                @pl.when(col == bend)
                def _():
                    detour_copy(hop, chunk).wait_send()

                @pl.when(col == last)
                def _():
                    relay_copy(hop, chunk).wait_send()
            else:
                @pl.when(first & (col < last))
                def _():
                    halo_copy(hop, chunk).wait_send()

    def sent(d, carry):
        peer = lax.rem(me + d, n)
        code_copy(peer, me).wait_send()
        kv_copy(peer, me).wait_send()
        q_copy(peer, me).wait_send()
        return carry

    lax.fori_loop(1, n, sent, 0)


def per_device(n, columns, queries, keys, values, dest_replica, dest_slot, doc_lengths, tile_mask):
    q = queries.reshape(NB, BLK, HEADS * WIDTH)
    k = keys.reshape(NB, BLK, WIDTH)
    v = values.reshape(NB, BLK, WIDTH)
    vmem, smem = pltpu.VMEM, pltpu.SMEM
    bf16, f32, i32 = jnp.bfloat16, jnp.float32, jnp.int32
    dma = pltpu.SemaphoreType.DMA
    out = pl.pallas_call(
        functools.partial(kernel, n, columns),
        out_shape=jax.ShapeDtypeStruct((NB, BLK, HEADS * WIDTH), bf16),
        in_specs=[pl.BlockSpec(memory_space=pltpu.HBM)] * 7,
        out_specs=pl.BlockSpec(memory_space=vmem),
        scratch_shapes=[
            vmem(q.shape, bf16), vmem(k.shape, bf16), vmem(v.shape, bf16),
            smem(dest_replica.shape, i32), vmem(dest_replica.shape, i32), vmem(dest_slot.shape, i32),
            vmem(doc_lengths.shape, i32), vmem(tile_mask.shape[1:], i32), dma((8,)),
            vmem((n, 2, BLK, WIDTH), bf16),
            vmem((n, 2, BLK, WIDTH), bf16),
            vmem((n, BLK, HEADS * WIDTH), bf16),
            vmem((n, BLK, HEADS * WIDTH), bf16),
            vmem((1, 128), i32),
            vmem((n, 1, 128), i32),
            vmem((3, NB, 2, BLK, WIDTH), bf16),
            vmem((2, NB, 2, BLK, WIDTH), bf16),
            vmem((NB, ROWS, 2 * WIDTH), bf16),
            vmem((3, TOK, 2 * WIDTH), bf16),
            vmem((3, TOK, 2 * WIDTH), bf16),
            vmem((NB, 16, 128), bf16),
            vmem((NB, ROWS, 2 * WIDTH), f32),
            vmem((NB, ROWS, 128), f32),
            vmem((PER, ROWS, 2 * WIDTH), f32),
            vmem((PER, ROWS, 128), f32),
            smem((NB,), i32), smem((NB,), i32), smem((NB,), i32),
            vmem((GROUP, TOK), f32), vmem((GROUP, 128), f32), vmem((GROUP, TOK), f32), vmem((GROUP, 128), f32),
            dma((n,)), dma((n,)), dma((n,)), dma((n,)), dma((n,)), dma((n,)),
            dma((2, CHUNKS)), dma((2, CHUNKS)), dma((2, CHUNKS)), dma((2, CHUNKS)), dma((2, CHUNKS)),
        ],
        compiler_params=pltpu.CompilerParams(
            collective_id=0, has_side_effects=True, vmem_limit_bytes=56 * 1024 * 1024),
        cost_estimate=pl.CostEstimate(flops=10**10, bytes_accessed=4 * 2**20, transcendentals=10**7),
    )(q, k, v, dest_replica, dest_slot, doc_lengths, tile_mask[0])
    return out.reshape(1, TOK, HEADS * WIDTH)


def solution(mesh):
    n, columns = mesh.shape["dp"], mesh.shape["ctx"]
    return jax.shard_map(
        functools.partial(per_device, n, columns),
        mesh=mesh,
        in_specs=(
            P("dp", "ctx", None),
            P("dp", "ctx", None),
            P("dp", "ctx", None),
            P("dp", "ctx"),
            P("dp", "ctx"),
            P("dp", None),
            P("dp", "ctx", None),
        ),
        out_specs=P("dp", "ctx", None),
        check_vma=False,
    )
```

```python
import functools

import jax
import jax.numpy as jnp
from jax import lax
from jax.experimental import pallas as pl
from jax.experimental.pallas import tpu as pltpu
from jax.sharding import PartitionSpec as P

MESH = pl.DeviceIdType.MESH
HEADS = 4
WIDTH = 128
BLK = 64
NB = 16
TOK = NB * BLK
ROWS = HEADS * BLK
KEYS = 256
SCALE = WIDTH ** (-0.5) * 1.4426950408889634
LOW = -32768.0
CHUNKS = 4
PER = NB // CHUNKS
PAIR = 2
GROUP = PAIR * ROWS
ORDER = (3, 2, 1, 0)
BY_LAST = ((), (2, 1, 0))
STEPS = (
    (0, 0, 1), (1, 0, 0), (3, 0, 1), (0, 1, 0), (2, 1, 1),
    (1, 1, 0), (3, 1, 1), (2, 0, 0), (1, 0, 1), (3, 0, 0),
    (2, 1, 0), (1, 1, 1), (3, 1, 0), (2, 0, 1), (0, 1, 1),
)
BATCHES = ((1, 6), (6, 11), (11, 16))


def tile_bias(col, docs_ref, mask_ref):
    count = docs_ref.shape[1]
    blocks = mask_ref.shape[1]
    lengths = docs_ref[...].astype(jnp.float32)
    upto = lax.broadcasted_iota(jnp.int32, (count, count), 1) <= lax.broadcasted_iota(jnp.int32, (count, count), 0)
    ends = jnp.sum(jnp.where(upto, jnp.broadcast_to(lengths, (count, count)), 0.0), axis=1, keepdims=True)
    block = lax.broadcasted_iota(jnp.int32, (count, blocks), 1).astype(jnp.float32)
    key_doc = jnp.sum(jnp.where(ends <= block, 1.0, 0.0), axis=0, keepdims=True)
    key_doc = jnp.broadcast_to(key_doc, (NB, blocks))
    key_block = lax.broadcasted_iota(jnp.int32, (NB, blocks), 1)
    query_block = lax.broadcasted_iota(jnp.int32, (NB, blocks), 0) + col * NB
    own = key_block == query_block
    query_doc = jnp.sum(jnp.where(own, key_doc, 0.0), axis=1, keepdims=True)
    ok = (key_doc == query_doc) & (key_block <= query_block) & ((mask_ref[...] == 1) | own)
    ok = jnp.where(ok, 1.0, 0.0).astype(jnp.bfloat16)
    window = lax.broadcasted_iota(jnp.int32, (blocks, 128), 1) + (col - 2) * NB
    pick = jnp.where(lax.broadcasted_iota(jnp.int32, (blocks, 128), 0) == window, 1.0, 0.0).astype(jnp.bfloat16)
    ok = jnp.dot(ok, pick, preferred_element_type=jnp.float32)
    return ((1.0 - ok) * LOW).astype(jnp.bfloat16)


def kernel(
    n, columns, q_hbm, k_hbm, v_hbm, rep_hbm, slot_hbm, docs_hbm, mask_hbm, out_ref,
    q_ref, k_ref, v_ref, rep_ref, rep_vec, slot_vec, docs_ref, mask_ref, load_sem,
    kv_send, kv_recv, q_send, q_recv, code_send, code_recv, halo, relay, q_aug, k_aug, v_aug, bias, acc, top, acc_tail, top_tail, src, at, slot_of,
    score_a, high_a, score_b, high_b,
    kv_sent, kv_got, q_sent, q_got, code_sent, code_got, halo_sent, halo_got,
    detour_sent, detour_got, relay_sent,
):
    me = lax.axis_index("dp")
    col = lax.axis_index("ctx")
    last = columns - 1
    bend = columns // 2 - 1
    right = lax.rem(col + 1, columns)
    left = lax.rem(col + columns - 1, columns)

    spots = (me // 4, lax.rem(me // 2, 2), lax.rem(me, 2))

    def partner(d, sign):
        if d == 0:
            return me
        dx, dy, dc = STEPS[d - 1]
        x = lax.rem(spots[0] + (4 + sign * dx), 4)
        return (x * 2 + lax.rem(spots[1] + dy, 2)) * 2 + lax.rem(spots[2] + dc, 2)

    targets = [partner(d, 1) for d in range(n)]
    sources = [partner(d, -1) for d in range(n)]

    loads = [
        pltpu.make_async_copy(a, b, load_sem.at[i])
        for i, (a, b) in enumerate((
            (rep_hbm, rep_ref), (rep_hbm, rep_vec), (slot_hbm, slot_vec), (k_hbm, k_ref), (v_hbm, v_ref),
            (q_hbm, q_ref), (docs_hbm, docs_ref), (mask_hbm, mask_ref)))
    ]
    for load in loads:
        load.start()

    barrier = pltpu.get_barrier_semaphore()

    def greet(d, carry):
        pl.semaphore_signal(barrier, inc=1, device_id={"dp": lax.rem(me + d, n)}, device_id_type=MESH)
        return carry

    lax.fori_loop(1, n, greet, 0)

    @pl.when(col > 0)
    def _():
        pl.semaphore_signal(barrier, inc=1, device_id={"ctx": left}, device_id_type=MESH)

    for here, there in ((last, bend), (bend + 1, last)):
        @pl.when(col == here)
        def _():
            pl.semaphore_signal(barrier, inc=1, device_id={"ctx": there}, device_id_type=MESH)

    for load in loads[:5]:
        load.wait()
    code_send[...] = jnp.full((1, 128), -1, jnp.int32)
    code_send[:, :NB] = rep_vec[...] * NB + slot_vec[...] - col * NB

    def block_for(peer):
        where = jnp.int32(0)
        for j in range(NB):
            where = jnp.where(rep_ref[0, j] == peer, j, where)
        return where

    held = [block_for(peer) for peer in targets]
    for d in range(1, n):
        kv_send[targets[d], 0] = k_ref[held[d]]
        kv_send[targets[d], 1] = v_ref[held[d]]

    def kv_copy(peer, slot):
        return pltpu.make_async_remote_copy(
            src_ref=kv_send.at[peer], dst_ref=kv_recv.at[slot], send_sem=kv_sent.at[peer],
            recv_sem=kv_got.at[slot], device_id={"dp": peer}, device_id_type=MESH)

    def q_copy(peer, slot):
        return pltpu.make_async_remote_copy(
            src_ref=q_send.at[peer], dst_ref=q_recv.at[slot], send_sem=q_sent.at[peer],
            recv_sem=q_got.at[slot], device_id={"dp": peer}, device_id_type=MESH)

    def code_copy(peer, slot):
        return pltpu.make_async_remote_copy(
            src_ref=code_send, dst_ref=code_recv.at[slot], send_sem=code_sent.at[peer],
            recv_sem=code_got.at[slot], device_id={"dp": peer}, device_id_type=MESH)

    pl.semaphore_wait(barrier, n + jnp.where(col == bend, 1, 0))

    for d in range(1, n):
        code_copy(targets[d], me).start()
        kv_copy(targets[d], me).start()
    loads[5].wait()

    def send_q(batch):
        for d in range(*BATCHES[batch]):
            q_send[targets[d]] = q_ref[held[d]]
            q_copy(targets[d], me).start()

    send_q(0)
    early = (col == 0) | (col == bend) | (col == bend + 1)

    @pl.when(early)
    def _():
        send_q(1)
        send_q(2)

    mine = held[0]
    q_recv[me] = q_ref[mine]
    kv_recv[me, 0] = k_ref[mine]
    kv_recv[me, 1] = v_ref[mine]
    code_recv[me] = code_send[...]

    loads[6].wait()
    loads[7].wait()
    rows = tile_bias(col, docs_ref, mask_ref).astype(jnp.float32)
    for i in range(NB):
        bias[i] = jnp.broadcast_to(rows[i:i + 1], (16, 128)).astype(jnp.bfloat16)
    key_at = lax.broadcasted_iota(jnp.int32, (TOK, 128), 0) // BLK
    lane = lax.broadcasted_iota(jnp.int32, (TOK, 128), 1)
    for p in range(3):
        k_aug[p, :, WIDTH:] = jnp.where(lane == key_at + (2 - p) * NB, 1.0, 0.0).astype(jnp.bfloat16)
        v_aug[p, :, WIDTH:] = jnp.ones((TOK, 128), jnp.bfloat16)
    nothing = jnp.zeros((2, BLK, WIDTH), jnp.bfloat16)
    halo[2, 0] = nothing
    for hop in (1, 2):
        @pl.when(col < hop)
        def _():
            for i in range(NB):
                halo[hop, i] = nothing

    for d in range(1, n):
        code_copy(sources[d], sources[d]).wait_recv()
    codes = code_recv[...].reshape(n, 128)
    sender = lax.broadcasted_iota(jnp.int32, (n, 128), 0)
    for i in range(NB):
        source = jnp.max(jnp.where(codes == me * NB + i, sender, 0))
        src[i] = source
        order = jnp.int32(0)
        for d in range(1, n):
            order = jnp.where(source == sources[d], d, order)
        at[i] = order
    for d in range(n):
        row = code_recv[sources[d]]
        slot_of[d] = jnp.max(jnp.where((row >= me * NB) & (row < (me + 1) * NB), row - me * NB, 0))
    for d in range(1, n):
        kv_copy(sources[d], sources[d]).wait_recv()

    def part_of(hop, chunk):
        return pl.ds(1, PER - 1) if hop == 1 and chunk == 0 else pl.ds(chunk * PER, PER)

    def halo_copy(hop, chunk):
        part = part_of(hop, chunk)
        return pltpu.make_async_remote_copy(
            src_ref=halo.at[hop, part], dst_ref=halo.at[hop + 1, part], send_sem=halo_sent.at[hop, chunk],
            recv_sem=halo_got.at[hop, chunk], device_id={"ctx": right}, device_id_type=MESH)

    def detour_of(hop, chunk):
        return last if chunk in BY_LAST[hop] else None

    def detour_copy(hop, chunk):
        part = part_of(hop, chunk)
        return pltpu.make_async_remote_copy(
            src_ref=halo.at[hop, part], dst_ref=relay.at[hop, part], send_sem=detour_sent.at[hop, chunk],
            recv_sem=detour_got.at[hop, chunk], device_id={"ctx": detour_of(hop, chunk)}, device_id_type=MESH)

    def relay_copy(hop, chunk):
        part = part_of(hop, chunk)
        return pltpu.make_async_remote_copy(
            src_ref=relay.at[hop, part], dst_ref=halo.at[hop + 1, part], send_sem=relay_sent.at[hop, chunk],
            recv_sem=halo_got.at[hop, chunk], device_id={"ctx": bend + 1}, device_id_type=MESH)

    def sends(hop, chunk):
        to_right = (col >= hop) & (col < last)
        if detour_of(hop, chunk) is not None:
            to_right = to_right & (col != bend)
        return to_right

    def send_halo(hop, chunk):
        @pl.when(sends(hop, chunk))
        def _():
            halo_copy(hop, chunk).start()

        if detour_of(hop, chunk) is not None:
            @pl.when(col == bend)
            def _():
                detour_copy(hop, chunk).start()

    def pass_on(hop, chunk):
        @pl.when(col == detour_of(hop, chunk))
        def _():
            detour_copy(hop, chunk).wait_recv()
            relay_copy(hop, chunk).start()

    def forward(chunk):
        @pl.when(col > 0)
        def _():
            halo_copy(0, chunk).wait_recv()

        if detour_of(1, chunk) is None:
            @pl.when(sends(1, chunk) & (col != bend))
            def _():
                halo_copy(1, chunk).start()
        else:
            send_halo(1, chunk)

    def cross(chunk):
        @pl.when(col == bend)
        def _():
            halo_copy(1, chunk).start()

    def place_kv(i, carry):
        s = src[i]
        rows = pl.ds(pl.multiple_of(i * BLK, BLK), BLK)
        key, value = kv_recv[s, 0], kv_recv[s, 1]
        halo[0, i, 0] = key
        halo[0, i, 1] = value
        k_aug[0, rows, :WIDTH] = key
        v_aug[0, rows, :WIDTH] = value
        return carry

    for chunk in ORDER:
        lax.fori_loop(chunk * PER, (chunk + 1) * PER, place_kv, 0)
        send_halo(0, chunk)

    def got_q(d):
        q_copy(sources[d], sources[d]).wait_recv()

    def wide(value, width):
        return jnp.concatenate([value] * (width // 128), axis=1)

    def score(p, i, lo, hi, buffer, high):
        if p == 0:
            parts = []
            for b in range(PAIR):
                block = q_recv[sources[i + b]]
                rows = bias[slot_of[i + b]]
                heads = jnp.concatenate([block[:, h * WIDTH:(h + 1) * WIDTH] for h in range(HEADS)], axis=0)
                part = jnp.concatenate([heads, jnp.concatenate([rows] * (ROWS // 16), axis=0)], axis=1)
                q_aug[i + b] = part
                parts.append(part)
            query = jnp.concatenate(parts, axis=0)
        elif p == 1:
            query = q_aug[pl.ds(i, PAIR)].reshape(GROUP, 2 * WIDTH)
        else:
            query = jnp.concatenate([q_aug[at[i + b]] for b in range(PAIR)], axis=0)
        width = hi - lo
        value = lax.dot_general(
            query, k_aug[min(p, 2), lo:hi, :], (((1,), (1,)), ((), ())), preferred_element_type=jnp.float32)
        if p == 0:
            row = lax.broadcasted_iota(jnp.int32, (GROUP, 128), 0)
            upto = lax.rem(row, BLK) + jnp.where(row < ROWS, slot_of[i], slot_of[i + 1]) * BLK
            key = lax.broadcasted_iota(jnp.int32, (GROUP, TOK), 1)
            value = jnp.where(key <= wide(upto, TOK), value, LOW)
        buffer[:, :width] = value
        most = value[:, :128]
        for c in range(128, width, 128):
            most = jnp.maximum(most, value[:, c:c + 128])
        high[...] = jnp.broadcast_to(jnp.max(most, axis=1, keepdims=True), (GROUP, 128))

    def finish(i, part):
        result = (part[:, :WIDTH] / part[:, WIDTH:]).astype(jnp.bfloat16)
        for b in range(PAIR):
            for h in range(HEADS):
                first = b * ROWS + h * BLK
                out_ref[i + b, :, h * WIDTH:(h + 1) * WIDTH] = result[first:first + BLK]

    def soft(p, i, lo, hi, buffer, high):
        width = hi - lo
        most = high[...]
        total = None
        if p == 1:
            before = top[pl.ds(i, PAIR)].reshape(GROUP, 128)
            total = acc[pl.ds(i, PAIR)].reshape(GROUP, 2 * WIDTH)
        elif p in (2, 3):
            before = jnp.concatenate([top[at[i + b]] for b in range(PAIR)], axis=0)
            total = jnp.concatenate([acc[at[i + b]] for b in range(PAIR)], axis=0)
        elif p == 4:
            before = top_tail[pl.ds(i, PAIR)].reshape(GROUP, 128)
            total = acc_tail[pl.ds(i, PAIR)].reshape(GROUP, 2 * WIDTH)
        if total is not None:
            most = jnp.maximum(most, before)
        weight = jnp.exp2((buffer[:, :width] - wide(most, width)) * SCALE)
        part = jnp.dot(
            weight.astype(jnp.bfloat16), v_aug[min(p, 2), lo:hi, :], preferred_element_type=jnp.float32)
        if total is not None:
            factor = jnp.exp2((before - most) * SCALE)
            part = part + total * wide(factor, 2 * WIDTH)
        if p < 2:
            acc[pl.ds(i, PAIR)] = part.reshape(PAIR, ROWS, 2 * WIDTH)
            top[pl.ds(i, PAIR)] = most.reshape(PAIR, ROWS, 128)
        elif p == 3:
            acc_tail[pl.ds(i, PAIR)] = part.reshape(PAIR, ROWS, 2 * WIDTH)
            top_tail[pl.ds(i, PAIR)] = most.reshape(PAIR, ROWS, 128)
        else:
            finish(i, part)

    def take_halo(hop, chunk):
        for i in range(chunk * PER, (chunk + 1) * PER):
            k_aug[hop, i * BLK:(i + 1) * BLK, :WIDTH] = halo[hop, i, 0]
            v_aug[hop, i * BLK:(i + 1) * BLK, :WIDTH] = halo[hop, i, 1]

    def second(chunk):
        @pl.when(col > 1)
        def _():
            halo_copy(1, chunk).wait_recv()
        take_halo(2, chunk)

    def arrive():
        for chunk in ORDER:
            take_halo(1, chunk)

    steps = [(0, i, 0, TOK) for i in range(0, NB, PAIR)]
    count = len(steps)
    steps += [(1, i, 0, TOK) for i in range(0, NB, PAIR)]
    steps += [(2, i, min((i + 1) // PER, 3) * KEYS, TOK) for i in range(NB - PAIR, PER - 1, -PAIR)]
    steps += [(3, i, KEYS, TOK) for i in range(PER - PAIR, -1, -PAIR)]
    final = len(steps)
    steps += [(4, i, 0, KEYS) for i in range(PER - PAIR, -1, -PAIR)]
    before = {k: [] for k in range(len(steps))}
    for k in range(count):
        for b in range(PAIR):
            if k * PAIR + b:
                before[k].append(functools.partial(got_q, k * PAIR + b))
    @pl.when(jnp.logical_not(early))
    def _():
        send_q(1)

    for d in range(*BATCHES[0]):
        q_copy(targets[d], me).wait_send()

    @pl.when(jnp.logical_not(early))
    def _():
        send_q(2)

    forward(3)
    before[2] += [lambda: forward(2)]
    before[5] += [lambda: forward(1)]
    before[count] += [lambda: forward(0), lambda: cross(3), arrive]
    before[count + 1] += [lambda: pass_on(1, 2)]
    before[count + 3] += [lambda: pass_on(1, 1)]
    before[count + 6] += [lambda: pass_on(1, 0)]
    before[2 * count] += [lambda: second(3)]
    before[2 * count + 2] += [lambda: second(2)]
    before[2 * count + 4] += [lambda: second(1)]
    before[final] += [lambda: second(0)]
    buffers = ((score_a, high_a), (score_b, high_b))
    for act in before[0]:
        act()
    score(*steps[0], *buffers[0])
    k = 0
    while k < len(steps):
        for act in before.get(k + 1, ()):
            act()
        def advance(k=k):
            if k + 1 < len(steps):
                score(*steps[k + 1], *buffers[(k + 1) % 2])
            soft(*steps[k], *buffers[k % 2])

        if k < count:
            advance()
        else:
            pl.when(col > 0)(advance)
        k += 1

    @pl.when(col == 0)
    def _():
        def alone(j, carry):
            i = j * PAIR
            finish(i, jnp.concatenate([acc[at[i + b]] for b in range(PAIR)], axis=0))
            return carry

        lax.fori_loop(0, NB // PAIR, alone, 0)

    for hop in range(2):
        for chunk in range(CHUNKS):
            @pl.when(sends(hop, chunk))
            def _():
                halo_copy(hop, chunk).wait_send()

            via = detour_of(hop, chunk)
            if via is not None:
                @pl.when(col == bend)
                def _():
                    detour_copy(hop, chunk).wait_send()

                @pl.when(col == via)
                def _():
                    relay_copy(hop, chunk).wait_send()

    for d in range(1, n):
        code_copy(targets[d], me).wait_send()
        kv_copy(targets[d], me).wait_send()
    for d in range(BATCHES[1][0], n):
        q_copy(targets[d], me).wait_send()


def per_device(n, columns, queries, keys, values, dest_replica, dest_slot, doc_lengths, tile_mask):
    q = queries.reshape(NB, BLK, HEADS * WIDTH)
    k = keys.reshape(NB, BLK, WIDTH)
    v = values.reshape(NB, BLK, WIDTH)
    vmem, smem = pltpu.VMEM, pltpu.SMEM
    bf16, f32, i32 = jnp.bfloat16, jnp.float32, jnp.int32
    dma = pltpu.SemaphoreType.DMA
    out = pl.pallas_call(
        functools.partial(kernel, n, columns),
        out_shape=jax.ShapeDtypeStruct((NB, BLK, HEADS * WIDTH), bf16),
        in_specs=[pl.BlockSpec(memory_space=pltpu.HBM)] * 7,
        out_specs=pl.BlockSpec(memory_space=vmem),
        scratch_shapes=[
            vmem(q.shape, bf16), vmem(k.shape, bf16), vmem(v.shape, bf16),
            smem(dest_replica.shape, i32), vmem(dest_replica.shape, i32), vmem(dest_slot.shape, i32),
            vmem(doc_lengths.shape, i32), vmem(tile_mask.shape[1:], i32), dma((8,)),
            vmem((n, 2, BLK, WIDTH), bf16),
            vmem((n, 2, BLK, WIDTH), bf16),
            vmem((n, BLK, HEADS * WIDTH), bf16),
            vmem((n, BLK, HEADS * WIDTH), bf16),
            vmem((1, 128), i32),
            vmem((n, 1, 128), i32),
            vmem((3, NB, 2, BLK, WIDTH), bf16),
            vmem((2, NB, 2, BLK, WIDTH), bf16),
            vmem((NB, ROWS, 2 * WIDTH), bf16),
            vmem((3, TOK, 2 * WIDTH), bf16),
            vmem((3, TOK, 2 * WIDTH), bf16),
            vmem((NB, 16, 128), bf16),
            vmem((NB, ROWS, 2 * WIDTH), f32),
            vmem((NB, ROWS, 128), f32),
            vmem((PER, ROWS, 2 * WIDTH), f32),
            vmem((PER, ROWS, 128), f32),
            smem((NB,), i32), smem((NB,), i32), smem((NB,), i32),
            vmem((GROUP, TOK), f32), vmem((GROUP, 128), f32), vmem((GROUP, TOK), f32), vmem((GROUP, 128), f32),
            dma((n,)), dma((n,)), dma((n,)), dma((n,)), dma((n,)), dma((n,)),
            dma((2, CHUNKS)), dma((2, CHUNKS)), dma((2, CHUNKS)), dma((2, CHUNKS)), dma((2, CHUNKS)),
        ],
        compiler_params=pltpu.CompilerParams(
            collective_id=0, has_side_effects=True, vmem_limit_bytes=56 * 1024 * 1024),
        cost_estimate=pl.CostEstimate(flops=10**10, bytes_accessed=4 * 2**20, transcendentals=10**7),
    )(q, k, v, dest_replica, dest_slot, doc_lengths, tile_mask[0])
    return out.reshape(1, TOK, HEADS * WIDTH)


def solution(mesh):
    n, columns = mesh.shape["dp"], mesh.shape["ctx"]
    return jax.shard_map(
        functools.partial(per_device, n, columns),
        mesh=mesh,
        in_specs=(
            P("dp", "ctx", None),
            P("dp", "ctx", None),
            P("dp", "ctx", None),
            P("dp", "ctx"),
            P("dp", "ctx"),
            P("dp", None),
            P("dp", "ctx", None),
        ),
        out_specs=P("dp", "ctx", None),
        check_vma=False,
    )
```

```python
import functools

import jax
import jax.numpy as jnp
from jax import lax
from jax.experimental import pallas as pl
from jax.experimental.pallas import tpu as pltpu
from jax.sharding import PartitionSpec as P

MESH = pl.DeviceIdType.MESH
HEADS = 4
WIDTH = 128
BLK = 64
NB = 16
TOK = NB * BLK
ROWS = HEADS * BLK
KEYS = 256
SCALE = WIDTH ** (-0.5) * 1.4426950408889634
LOW = -32768.0
CHUNKS = 4
PER = NB // CHUNKS
PAIR = 2
GROUP = PAIR * ROWS
ORDER = (3, 2, 1, 0)
BY_LAST = ((), (1, 0))
STEPS = (
    (0, 0, 1), (1, 0, 0), (3, 0, 1), (0, 1, 0), (2, 1, 1),
    (1, 1, 0), (3, 1, 1), (2, 0, 0), (1, 0, 1), (3, 0, 0),
    (2, 1, 0), (1, 1, 1), (3, 1, 0), (2, 0, 1), (0, 1, 1),
)
BATCHES = ((1, 6), (6, 11), (11, 16))


def tile_bias(col, docs_ref, mask_ref):
    count = docs_ref.shape[1]
    blocks = mask_ref.shape[1]
    lengths = docs_ref[...].astype(jnp.float32)
    upto = lax.broadcasted_iota(jnp.int32, (count, count), 1) <= lax.broadcasted_iota(jnp.int32, (count, count), 0)
    ends = jnp.sum(jnp.where(upto, jnp.broadcast_to(lengths, (count, count)), 0.0), axis=1, keepdims=True)
    block = lax.broadcasted_iota(jnp.int32, (count, blocks), 1).astype(jnp.float32)
    key_doc = jnp.sum(jnp.where(ends <= block, 1.0, 0.0), axis=0, keepdims=True)
    key_doc = jnp.broadcast_to(key_doc, (NB, blocks))
    key_block = lax.broadcasted_iota(jnp.int32, (NB, blocks), 1)
    query_block = lax.broadcasted_iota(jnp.int32, (NB, blocks), 0) + col * NB
    own = key_block == query_block
    query_doc = jnp.sum(jnp.where(own, key_doc, 0.0), axis=1, keepdims=True)
    ok = (key_doc == query_doc) & (key_block <= query_block) & ((mask_ref[...] == 1) | own)
    ok = jnp.where(ok, 1.0, 0.0).astype(jnp.bfloat16)
    window = lax.broadcasted_iota(jnp.int32, (blocks, 128), 1) + (col - 2) * NB
    pick = jnp.where(lax.broadcasted_iota(jnp.int32, (blocks, 128), 0) == window, 1.0, 0.0).astype(jnp.bfloat16)
    ok = jnp.dot(ok, pick, preferred_element_type=jnp.float32)
    return ((1.0 - ok) * LOW).astype(jnp.bfloat16)


def kernel(
    n, columns, q_hbm, k_hbm, v_hbm, rep_hbm, slot_hbm, docs_hbm, mask_hbm, out_ref,
    q_ref, k_ref, v_ref, rep_ref, rep_vec, slot_vec, docs_ref, mask_ref, load_sem,
    kv_send, kv_recv, q_send, q_recv, code_send, code_recv, halo, relay, q_aug, k_aug, v_aug, bias, acc, top, acc_tail, top_tail, src, at, slot_of,
    score_a, high_a, score_b, high_b,
    kv_sent, kv_got, q_sent, q_got, code_sent, code_got, halo_sent, halo_got,
    detour_sent, detour_got, relay_sent,
):
    me = lax.axis_index("dp")
    col = lax.axis_index("ctx")
    last = columns - 1
    bend = columns // 2 - 1
    right = lax.rem(col + 1, columns)
    left = lax.rem(col + columns - 1, columns)

    spots = (me // 4, lax.rem(me // 2, 2), lax.rem(me, 2))

    def partner(d, sign):
        if d == 0:
            return me
        dx, dy, dc = STEPS[d - 1]
        x = lax.rem(spots[0] + (4 + sign * dx), 4)
        return (x * 2 + lax.rem(spots[1] + dy, 2)) * 2 + lax.rem(spots[2] + dc, 2)

    targets = [partner(d, 1) for d in range(n)]
    sources = [partner(d, -1) for d in range(n)]

    loads = [
        pltpu.make_async_copy(a, b, load_sem.at[i])
        for i, (a, b) in enumerate((
            (rep_hbm, rep_ref), (rep_hbm, rep_vec), (slot_hbm, slot_vec), (k_hbm, k_ref), (v_hbm, v_ref),
            (q_hbm, q_ref), (docs_hbm, docs_ref), (mask_hbm, mask_ref)))
    ]
    for load in loads:
        load.start()

    barrier = pltpu.get_barrier_semaphore()

    def greet(d, carry):
        pl.semaphore_signal(barrier, inc=1, device_id={"dp": lax.rem(me + d, n)}, device_id_type=MESH)
        return carry

    lax.fori_loop(1, n, greet, 0)

    @pl.when(col > 0)
    def _():
        pl.semaphore_signal(barrier, inc=1, device_id={"ctx": left}, device_id_type=MESH)

    for here, there in ((last, bend), (bend + 1, last)):
        @pl.when(col == here)
        def _():
            pl.semaphore_signal(barrier, inc=1, device_id={"ctx": there}, device_id_type=MESH)

    for load in loads[:5]:
        load.wait()
    code_send[...] = jnp.full((1, 128), -1, jnp.int32)
    code_send[:, :NB] = rep_vec[...] * NB + slot_vec[...] - col * NB

    def block_for(peer):
        where = jnp.int32(0)
        for j in range(NB):
            where = jnp.where(rep_ref[0, j] == peer, j, where)
        return where

    held = [block_for(peer) for peer in targets]
    for d in range(1, n):
        kv_send[targets[d], 0] = k_ref[held[d]]
        kv_send[targets[d], 1] = v_ref[held[d]]

    def kv_copy(peer, slot):
        return pltpu.make_async_remote_copy(
            src_ref=kv_send.at[peer], dst_ref=kv_recv.at[slot], send_sem=kv_sent.at[peer],
            recv_sem=kv_got.at[slot], device_id={"dp": peer}, device_id_type=MESH)

    def q_copy(peer, slot):
        return pltpu.make_async_remote_copy(
            src_ref=q_send.at[peer], dst_ref=q_recv.at[slot], send_sem=q_sent.at[peer],
            recv_sem=q_got.at[slot], device_id={"dp": peer}, device_id_type=MESH)

    def code_copy(peer, slot):
        return pltpu.make_async_remote_copy(
            src_ref=code_send, dst_ref=code_recv.at[slot], send_sem=code_sent.at[peer],
            recv_sem=code_got.at[slot], device_id={"dp": peer}, device_id_type=MESH)

    pl.semaphore_wait(barrier, n + jnp.where(col == bend, 1, 0))

    for d in range(1, n):
        code_copy(targets[d], me).start()
        kv_copy(targets[d], me).start()
    loads[5].wait()

    def send_q(batch):
        for d in range(*BATCHES[batch]):
            q_send[targets[d]] = q_ref[held[d]]
            q_copy(targets[d], me).start()

    send_q(0)
    early = (col == 0) | (col == bend) | (col == bend + 1)

    @pl.when(early)
    def _():
        send_q(1)
        send_q(2)

    mine = held[0]
    q_recv[me] = q_ref[mine]
    kv_recv[me, 0] = k_ref[mine]
    kv_recv[me, 1] = v_ref[mine]
    code_recv[me] = code_send[...]

    loads[6].wait()
    loads[7].wait()
    rows = tile_bias(col, docs_ref, mask_ref).astype(jnp.float32)
    for i in range(NB):
        bias[i] = jnp.broadcast_to(rows[i:i + 1], (16, 128)).astype(jnp.bfloat16)
    key_at = lax.broadcasted_iota(jnp.int32, (TOK, 128), 0) // BLK
    lane = lax.broadcasted_iota(jnp.int32, (TOK, 128), 1)
    for p in range(3):
        k_aug[p, :, WIDTH:] = jnp.where(lane == key_at + (2 - p) * NB, 1.0, 0.0).astype(jnp.bfloat16)
        v_aug[p, :, WIDTH:] = jnp.ones((TOK, 128), jnp.bfloat16)
    nothing = jnp.zeros((2, BLK, WIDTH), jnp.bfloat16)
    halo[2, 0] = nothing
    for hop in (1, 2):
        @pl.when(col < hop)
        def _():
            for i in range(NB):
                halo[hop, i] = nothing

    for d in range(1, n):
        code_copy(sources[d], sources[d]).wait_recv()
    codes = code_recv[...].reshape(n, 128)
    sender = lax.broadcasted_iota(jnp.int32, (n, 128), 0)
    for i in range(NB):
        source = jnp.max(jnp.where(codes == me * NB + i, sender, 0))
        src[i] = source
        order = jnp.int32(0)
        for d in range(1, n):
            order = jnp.where(source == sources[d], d, order)
        at[i] = order
    for d in range(n):
        row = code_recv[sources[d]]
        slot_of[d] = jnp.max(jnp.where((row >= me * NB) & (row < (me + 1) * NB), row - me * NB, 0))
    for d in range(1, n):
        kv_copy(sources[d], sources[d]).wait_recv()

    def part_of(hop, chunk):
        return pl.ds(1, PER - 1) if hop == 1 and chunk == 0 else pl.ds(chunk * PER, PER)

    def halo_copy(hop, chunk):
        part = part_of(hop, chunk)
        return pltpu.make_async_remote_copy(
            src_ref=halo.at[hop, part], dst_ref=halo.at[hop + 1, part], send_sem=halo_sent.at[hop, chunk],
            recv_sem=halo_got.at[hop, chunk], device_id={"ctx": right}, device_id_type=MESH)

    def detour_of(hop, chunk):
        return last if chunk in BY_LAST[hop] else None

    def detour_copy(hop, chunk):
        part = part_of(hop, chunk)
        return pltpu.make_async_remote_copy(
            src_ref=halo.at[hop, part], dst_ref=relay.at[hop, part], send_sem=detour_sent.at[hop, chunk],
            recv_sem=detour_got.at[hop, chunk], device_id={"ctx": detour_of(hop, chunk)}, device_id_type=MESH)

    def relay_copy(hop, chunk):
        part = part_of(hop, chunk)
        return pltpu.make_async_remote_copy(
            src_ref=relay.at[hop, part], dst_ref=halo.at[hop + 1, part], send_sem=relay_sent.at[hop, chunk],
            recv_sem=halo_got.at[hop, chunk], device_id={"ctx": bend + 1}, device_id_type=MESH)

    def sends(hop, chunk):
        to_right = (col >= hop) & (col < last)
        if detour_of(hop, chunk) is not None:
            to_right = to_right & (col != bend)
        return to_right

    def send_halo(hop, chunk):
        @pl.when(sends(hop, chunk))
        def _():
            halo_copy(hop, chunk).start()

        if detour_of(hop, chunk) is not None:
            @pl.when(col == bend)
            def _():
                detour_copy(hop, chunk).start()

    def pass_on(hop, chunk):
        @pl.when(col == detour_of(hop, chunk))
        def _():
            detour_copy(hop, chunk).wait_recv()
            relay_copy(hop, chunk).start()

    def forward(chunk, here=None):
        @pl.when(col > 0 if here is None else (col > 0) & here)
        def _():
            halo_copy(0, chunk).wait_recv()

        right_now = sends(1, chunk) & (col != bend)
        @pl.when(right_now if here is None else right_now & here)
        def _():
            halo_copy(1, chunk).start()

        if detour_of(1, chunk) is not None:
            @pl.when(col == bend if here is None else (col == bend) & here)
            def _():
                detour_copy(1, chunk).start()

    def cross(chunk):
        @pl.when(col == bend)
        def _():
            halo_copy(1, chunk).start()

    def place_kv(i, carry):
        s = src[i]
        rows = pl.ds(pl.multiple_of(i * BLK, BLK), BLK)
        key, value = kv_recv[s, 0], kv_recv[s, 1]
        halo[0, i, 0] = key
        halo[0, i, 1] = value
        k_aug[0, rows, :WIDTH] = key
        v_aug[0, rows, :WIDTH] = value
        return carry

    for chunk in ORDER:
        lax.fori_loop(chunk * PER, (chunk + 1) * PER, place_kv, 0)
        if chunk in (3, 2):
            send_halo(0, chunk)
        else:
            @pl.when(sends(0, chunk) & (col != bend))
            def _():
                halo_copy(0, chunk).start()

    def second_part():
        @pl.when(col == bend)
        def _():
            for chunk in (3, 2):
                halo_copy(0, chunk).wait_send()
            for chunk in (1, 0):
                halo_copy(0, chunk).start()

    def got_q(d):
        q_copy(sources[d], sources[d]).wait_recv()

    def wide(value, width):
        return jnp.concatenate([value] * (width // 128), axis=1)

    def score(p, i, lo, hi, buffer, high):
        if p == 0:
            parts = []
            for b in range(PAIR):
                block = q_recv[sources[i + b]]
                rows = bias[slot_of[i + b]]
                heads = jnp.concatenate([block[:, h * WIDTH:(h + 1) * WIDTH] for h in range(HEADS)], axis=0)
                part = jnp.concatenate([heads, jnp.concatenate([rows] * (ROWS // 16), axis=0)], axis=1)
                q_aug[i + b] = part
                parts.append(part)
            query = jnp.concatenate(parts, axis=0)
        elif p == 1:
            query = q_aug[pl.ds(i, PAIR)].reshape(GROUP, 2 * WIDTH)
        else:
            query = jnp.concatenate([q_aug[at[i + b]] for b in range(PAIR)], axis=0)
        width = hi - lo
        value = lax.dot_general(
            query, k_aug[min(p, 2), lo:hi, :], (((1,), (1,)), ((), ())), preferred_element_type=jnp.float32)
        if p == 0:
            row = lax.broadcasted_iota(jnp.int32, (GROUP, 128), 0)
            upto = lax.rem(row, BLK) + jnp.where(row < ROWS, slot_of[i], slot_of[i + 1]) * BLK
            key = lax.broadcasted_iota(jnp.int32, (GROUP, TOK), 1)
            value = jnp.where(key <= wide(upto, TOK), value, LOW)
        buffer[:, :width] = value
        most = value[:, :128]
        for c in range(128, width, 128):
            most = jnp.maximum(most, value[:, c:c + 128])
        high[...] = jnp.broadcast_to(jnp.max(most, axis=1, keepdims=True), (GROUP, 128))

    def finish(i, part):
        result = (part[:, :WIDTH] / part[:, WIDTH:]).astype(jnp.bfloat16)
        for b in range(PAIR):
            for h in range(HEADS):
                first = b * ROWS + h * BLK
                out_ref[i + b, :, h * WIDTH:(h + 1) * WIDTH] = result[first:first + BLK]

    def soft(p, i, lo, hi, buffer, high):
        width = hi - lo
        most = high[...]
        total = None
        if p == 1:
            before = top[pl.ds(i, PAIR)].reshape(GROUP, 128)
            total = acc[pl.ds(i, PAIR)].reshape(GROUP, 2 * WIDTH)
        elif p in (2, 3):
            before = jnp.concatenate([top[at[i + b]] for b in range(PAIR)], axis=0)
            total = jnp.concatenate([acc[at[i + b]] for b in range(PAIR)], axis=0)
        elif p == 4:
            before = top_tail[pl.ds(i, PAIR)].reshape(GROUP, 128)
            total = acc_tail[pl.ds(i, PAIR)].reshape(GROUP, 2 * WIDTH)
        if total is not None:
            most = jnp.maximum(most, before)
        weight = jnp.exp2((buffer[:, :width] - wide(most, width)) * SCALE)
        part = jnp.dot(
            weight.astype(jnp.bfloat16), v_aug[min(p, 2), lo:hi, :], preferred_element_type=jnp.float32)
        if total is not None:
            factor = jnp.exp2((before - most) * SCALE)
            part = part + total * wide(factor, 2 * WIDTH)
        if p < 2:
            acc[pl.ds(i, PAIR)] = part.reshape(PAIR, ROWS, 2 * WIDTH)
            top[pl.ds(i, PAIR)] = most.reshape(PAIR, ROWS, 128)
        elif p == 3:
            acc_tail[pl.ds(i, PAIR)] = part.reshape(PAIR, ROWS, 2 * WIDTH)
            top_tail[pl.ds(i, PAIR)] = most.reshape(PAIR, ROWS, 128)
        else:
            finish(i, part)

    def take_halo(hop, chunk):
        for i in range(chunk * PER, (chunk + 1) * PER):
            k_aug[hop, i * BLK:(i + 1) * BLK, :WIDTH] = halo[hop, i, 0]
            v_aug[hop, i * BLK:(i + 1) * BLK, :WIDTH] = halo[hop, i, 1]

    def second(chunk):
        @pl.when(col > 1)
        def _():
            halo_copy(1, chunk).wait_recv()
        take_halo(2, chunk)

    def arrive(*chunks):
        for chunk in chunks:
            take_halo(1, chunk)

    steps = [(0, i, 0, TOK) for i in range(0, NB, PAIR)]
    count = len(steps)
    half = TOK // 2
    steps += [(1, i, half, TOK) for i in range(0, NB, PAIR)] + [(1, i, 0, half) for i in range(0, NB, PAIR)]
    other = len(steps)
    steps += [(2, i, min((i + 1) // PER, 3) * KEYS, TOK) for i in range(NB - PAIR, PER - 1, -PAIR)]
    steps += [(3, i, KEYS, TOK) for i in range(PER - PAIR, -1, -PAIR)]
    final = len(steps)
    steps += [(4, i, 0, KEYS) for i in range(PER - PAIR, -1, -PAIR)]
    before = {k: [] for k in range(len(steps))}
    for k in range(count):
        for b in range(PAIR):
            if k * PAIR + b:
                before[k].append(functools.partial(got_q, k * PAIR + b))
    @pl.when(jnp.logical_not(early))
    def _():
        send_q(1)

    for d in range(*BATCHES[0]):
        q_copy(targets[d], me).wait_send()

    @pl.when(jnp.logical_not(early))
    def _():
        send_q(2)

    forward(3, col != bend + 1)
    far = col == bend + 1
    near = col != bend + 1
    before[2] += [lambda: forward(2, near)]
    before[5] += [lambda: forward(1, near)]
    before[6] += [lambda: forward(3, far)]
    before[7] += [lambda: forward(2, far)]
    before[2] += [second_part]
    before[count] += [lambda: forward(0, near), lambda: cross(3), lambda: cross(2), lambda: arrive(3, 2)]
    before[count + 6] += [lambda: pass_on(1, 1)]
    before[count + 8] += [lambda: forward(1, far), lambda: forward(0, far), lambda: arrive(1, 0)]
    before[count + 11] += [lambda: pass_on(1, 0)]
    before[other] += [lambda: second(3)]
    before[other + 2] += [lambda: second(2)]
    before[other + 4] += [lambda: second(1)]
    before[final] += [lambda: second(0)]
    buffers = ((score_a, high_a), (score_b, high_b))
    for act in before[0]:
        act()
    score(*steps[0], *buffers[0])
    k = 0
    while k < len(steps):
        for act in before.get(k + 1, ()):
            act()
        def advance(k=k):
            if k + 1 < len(steps):
                score(*steps[k + 1], *buffers[(k + 1) % 2])
            soft(*steps[k], *buffers[k % 2])

        if k < count:
            advance()
        else:
            pl.when(col > 0)(advance)
        k += 1

    @pl.when(col == 0)
    def _():
        def alone(j, carry):
            i = j * PAIR
            finish(i, jnp.concatenate([acc[at[i + b]] for b in range(PAIR)], axis=0))
            return carry

        lax.fori_loop(0, NB // PAIR, alone, 0)

    for hop in range(2):
        for chunk in range(CHUNKS):
            taken = hop == 0 and chunk in (3, 2)

            @pl.when(sends(hop, chunk) & (col != bend) if taken else sends(hop, chunk))
            def _():
                halo_copy(hop, chunk).wait_send()

            via = detour_of(hop, chunk)
            if via is not None:
                @pl.when(col == bend)
                def _():
                    detour_copy(hop, chunk).wait_send()

                @pl.when(col == via)
                def _():
                    relay_copy(hop, chunk).wait_send()

    for d in range(1, n):
        code_copy(targets[d], me).wait_send()
        kv_copy(targets[d], me).wait_send()
    for d in range(BATCHES[1][0], n):
        q_copy(targets[d], me).wait_send()


def per_device(n, columns, queries, keys, values, dest_replica, dest_slot, doc_lengths, tile_mask):
    q = queries.reshape(NB, BLK, HEADS * WIDTH)
    k = keys.reshape(NB, BLK, WIDTH)
    v = values.reshape(NB, BLK, WIDTH)
    vmem, smem = pltpu.VMEM, pltpu.SMEM
    bf16, f32, i32 = jnp.bfloat16, jnp.float32, jnp.int32
    dma = pltpu.SemaphoreType.DMA
    out = pl.pallas_call(
        functools.partial(kernel, n, columns),
        out_shape=jax.ShapeDtypeStruct((NB, BLK, HEADS * WIDTH), bf16),
        in_specs=[pl.BlockSpec(memory_space=pltpu.HBM)] * 7,
        out_specs=pl.BlockSpec(memory_space=vmem),
        scratch_shapes=[
            vmem(q.shape, bf16), vmem(k.shape, bf16), vmem(v.shape, bf16),
            smem(dest_replica.shape, i32), vmem(dest_replica.shape, i32), vmem(dest_slot.shape, i32),
            vmem(doc_lengths.shape, i32), vmem(tile_mask.shape[1:], i32), dma((8,)),
            vmem((n, 2, BLK, WIDTH), bf16),
            vmem((n, 2, BLK, WIDTH), bf16),
            vmem((n, BLK, HEADS * WIDTH), bf16),
            vmem((n, BLK, HEADS * WIDTH), bf16),
            vmem((1, 128), i32),
            vmem((n, 1, 128), i32),
            vmem((3, NB, 2, BLK, WIDTH), bf16),
            vmem((2, NB, 2, BLK, WIDTH), bf16),
            vmem((NB, ROWS, 2 * WIDTH), bf16),
            vmem((3, TOK, 2 * WIDTH), bf16),
            vmem((3, TOK, 2 * WIDTH), bf16),
            vmem((NB, 16, 128), bf16),
            vmem((NB, ROWS, 2 * WIDTH), f32),
            vmem((NB, ROWS, 128), f32),
            vmem((PER, ROWS, 2 * WIDTH), f32),
            vmem((PER, ROWS, 128), f32),
            smem((NB,), i32), smem((NB,), i32), smem((NB,), i32),
            vmem((GROUP, TOK), f32), vmem((GROUP, 128), f32), vmem((GROUP, TOK), f32), vmem((GROUP, 128), f32),
            dma((n,)), dma((n,)), dma((n,)), dma((n,)), dma((n,)), dma((n,)),
            dma((2, CHUNKS)), dma((2, CHUNKS)), dma((2, CHUNKS)), dma((2, CHUNKS)), dma((2, CHUNKS)),
        ],
        compiler_params=pltpu.CompilerParams(
            collective_id=0, has_side_effects=True, vmem_limit_bytes=56 * 1024 * 1024),
        cost_estimate=pl.CostEstimate(flops=10**10, bytes_accessed=4 * 2**20, transcendentals=10**7),
    )(q, k, v, dest_replica, dest_slot, doc_lengths, tile_mask[0])
    return out.reshape(1, TOK, HEADS * WIDTH)


def solution(mesh):
    n, columns = mesh.shape["dp"], mesh.shape["ctx"]
    return jax.shard_map(
        functools.partial(per_device, n, columns),
        mesh=mesh,
        in_specs=(
            P("dp", "ctx", None),
            P("dp", "ctx", None),
            P("dp", "ctx", None),
            P("dp", "ctx"),
            P("dp", "ctx"),
            P("dp", None),
            P("dp", "ctx", None),
        ),
        out_specs=P("dp", "ctx", None),
        check_vma=False,
    )
```
